32 devices in a mesh: seq: 8 (over z, x), head: 4 (over y, core).
Axes of the slice: x: 2, y: 2, z: 4, core: 2. Of those that a mesh axis runs over, the one named last changes fastest.
Arguments:
- tokens: bfloat16 [8192, 2048], P('seq', 'head'), may hold values from -6 to 6
- norm_gain: bfloat16 [2048], P('head'), may hold values from 0.5 to 1.5
- w_query: bfloat16 [2048, 2048], P(None, 'head'), may hold values from -0.125 to 0.125
- w_key: bfloat16 [2048, 2048], P(None, 'head'), may hold values from -0.125 to 0.125
- w_value: bfloat16 [2048, 3456], P(None, 'head'), may hold values from -0.125 to 0.125
- w_gate: bfloat16 [2048, 3456], P(None, 'head'), may hold values from -0.125 to 0.125
- group_gain: bfloat16 [3456], P('head'), may hold values from 0.5 to 1.5
- w_output: bfloat16 [3456, 2048], P('head'), may hold values from -0.109375 to 0.109375
- mlp_gain: bfloat16 [2048], P('head'), may hold values from 0.5 to 1.5
- w_first: bfloat16 [2048, 3456], P(None, 'head'), may hold values from -0.125 to 0.125
- w_second: bfloat16 [2048, 3456], P(None, 'head'), may hold values from -0.125 to 0.125
- w_third: bfloat16 [3456, 2048], P('head'), may hold values from -0.109375 to 0.109375
- cotangent: bfloat16 [8192, 2048], P('seq', 'head'), may hold values from -6 to 6
Outputs:
- output: bfloat16 [8192, 2048], P('seq', 'head')
- grad_tokens: bfloat16 [8192, 2048], P('seq', 'head')
- grad_norm_gain: float32 [2048], P('head')
- grad_query: float32 [2048, 2048], P(None, 'head')
- grad_key: float32 [2048, 2048], P(None, 'head')
- grad_value: float32 [2048, 3456], P(None, 'head')
- grad_gate: float32 [2048, 3456], P(None, 'head')
- grad_group_gain: float32 [3456], P('head')
- grad_output: float32 [3456, 2048], P('head')
- grad_mlp_gain: float32 [2048], P('head')
- grad_first: float32 [2048, 3456], P(None, 'head')
- grad_second: float32 [2048, 3456], P(None, 'head')
- grad_third: float32 [3456, 2048], P('head')
The draws below stay inside these ranges and needn't reach their ends.
All inputs are finite; a program needn't handle non-finite values.
Results may differ from the reference program's by a relative error of at most 0.023.
Values may be sent and summed in bfloat16 or wider, within the bound.
A program may use at most 320 MiB of HBM per device.

```python
import math
import jax
import jax.numpy as jnp
from jax import lax

D = 2048
H = 8
DK = 256
DV = 432
FF = 3456
BLK = 512
TOKENS = 8192


def level_of(key, dims, split, smallest, largest):
    loudness, own = 1.0, jax.random.fold_in(key, 6)
    for position, shards_of in split:
        draws = jnp.exp(jax.random.uniform(jax.random.fold_in(own, position), (shards_of,), jnp.float32, smallest / len(split), largest / len(split)))
        loudness = loudness * jnp.repeat(draws, dims[position] // shards_of).reshape([-1 if axis == position else 1 for axis in range(len(dims))])
    return loudness


def bell_draw(rng, extent, spread, bound, cuts=(), kind=jnp.bfloat16):
    entries = spread * jax.random.normal(rng, extent, jnp.float32)
    if cuts:
        entries = entries * level_of(rng, extent, cuts, -0.22, 0.18)
    return jnp.clip(entries, -bound, bound).astype(kind)


def setup_inputs(seed: int = 0) -> dict:
    arg_keys = jax.random.split(jax.random.key(seed), 14)
    return {
        "tokens": bell_draw(arg_keys[0], (TOKENS, D), 1.0, 6.0, ((0, 8), (1, 4))),
        "norm_gain": jnp.clip(1.0 + 0.1 * jax.random.normal(arg_keys[1], (D,), jnp.float32), 0.5, 1.5).astype(jnp.bfloat16),
        "w_query": bell_draw(arg_keys[2], (D, H * DK), D ** -0.5, 0.125, ((1, 4),)),
        "w_key": bell_draw(arg_keys[3], (D, H * DK), D ** -0.5, 0.125, ((1, 4),)),
        "w_value": bell_draw(arg_keys[4], (D, H * DV), D ** -0.5, 0.125, ((1, 4),)),
        "w_gate": bell_draw(arg_keys[5], (D, H * DV), D ** -0.5, 0.125, ((1, 4),)),
        "group_gain": jnp.clip(1.0 + 0.1 * jax.random.normal(arg_keys[6], (H * DV,), jnp.float32), 0.5, 1.5).astype(jnp.bfloat16),
        "w_output": bell_draw(arg_keys[7], (H * DV, D), (H * DV) ** -0.5, 0.109375, ((0, 4),)),
        "mlp_gain": jnp.clip(1.0 + 0.1 * jax.random.normal(arg_keys[8], (D,), jnp.float32), 0.5, 1.5).astype(jnp.bfloat16),
        "w_first": bell_draw(arg_keys[9], (D, FF), D ** -0.5, 0.125, ((1, 4),)),
        "w_second": bell_draw(arg_keys[10], (D, FF), D ** -0.5, 0.125, ((1, 4),)),
        "w_third": bell_draw(arg_keys[11], (FF, D), FF ** -0.5, 0.109375, ((0, 4),)),
        "cotangent": bell_draw(arg_keys[12], (TOKENS, D), 1.0, 6.0, ((0, 8), (1, 4))),
    }


@jax.custom_vjp
def low(v):
    return lax.optimization_barrier(v.astype(jnp.bfloat16)).astype(jnp.float32)

@jax.custom_vjp
def low_back(v):
    return v

def low_keep(v):
    return (low(v), None)

def low_pass(kept, grad):
    return (grad,)

def back_keep(v):
    return (v, None)

def back_low(kept, grad):
    return (low(grad),)
low.defvjp(low_keep, low_pass)
low_back.defvjp(back_keep, back_low)
highest_precision = lax.Precision.HIGHEST

def matmul(left_side, right_side):
    return jnp.dot(left_side, right_side, precision=highest_precision, preferred_element_type=jnp.float32)

def layer_norm(values, scales, epsilon):
    centred = values - lax.optimization_barrier(jnp.mean(values, axis=-1, keepdims=True))
    inverse = lax.rsqrt(lax.optimization_barrier(jnp.mean(centred * centred, axis=-1, keepdims=True)) + epsilon)
    return centred * inverse * scales

def rotate(values, angles):
    half_size = values.shape[-1] // 2
    cosine = jnp.cos(angles)[:, None, :]
    sine_part = jnp.sin(angles)[:, None, :]
    first_half = values[..., :half_size]
    second_half = values[..., half_size:]
    return jnp.concatenate([first_half * cosine - second_half * sine_part, second_half * cosine + first_half * sine_part], axis=-1)

def gelu_exact(values):
    return 0.5 * values * (1.0 + jax.scipy.special.erf(values / math.sqrt(2.0)))

def retention(queries, key_rows, value_rows):
    head_ids = jnp.arange(H, dtype=jnp.float32)
    log_decay = jnp.log(1.0 - jnp.exp2(-5.0 - head_ids))
    offsets = jnp.arange(BLK, dtype=jnp.float32)
    lagged = offsets[:, None] - offsets[None, :]
    causal = lagged >= 0
    decay_mask = jnp.where(causal[None], jnp.exp(jnp.where(causal, lagged, 0.0)[None] * log_decay[:, None, None]), 0.0)
    into_block = jnp.exp((offsets[:, None] + 1.0) * log_decay[None, :])
    output_block_rows = jnp.exp((BLK - 1.0 - offsets)[:, None] * log_decay[None, :])
    across = jnp.exp(BLK * log_decay)

    def one_block(state, pieces):
        query_block_rows, key_block_rows, value_block_rows = pieces
        attention_scores = low_back(jnp.einsum('pvy,ovy->vpo', query_block_rows, key_block_rows, precision=highest_precision))
        weights = low(attention_scores * decay_mask)
        inner_part = jnp.einsum('hnm,mhe->nhe', weights, value_block_rows, precision=highest_precision)
        carried = jnp.einsum('nhd,hde->nhe', query_block_rows * into_block[:, :, None], state, precision=highest_precision)
        state_update = jnp.einsum('zrb,zrg->rbg', key_block_rows * output_block_rows[:, :, None], value_block_rows, precision=highest_precision)
        return (across[:, None, None] * state + state_update, inner_part + carried)
    blocks = TOKENS // BLK
    initial_state = jnp.zeros((H, DK, DV), jnp.float32)
    pieces = (queries.reshape(blocks, BLK, H, DK), key_rows.reshape(blocks, BLK, H, DK), value_rows.reshape(blocks, BLK, H, DV))
    _, outputs = lax.scan(jax.checkpoint(one_block), initial_state, pieces)
    return outputs.reshape(TOKENS, H, DV)

def forward(tokens, norm_gain, w_query, w_key, w_value, w_gate, group_gain, w_output, mlp_gain, w_first, w_second, w_third):
    positions = jnp.arange(TOKENS, dtype=jnp.float32)
    frequency = 10000.0 ** (-jnp.arange(DK // 2, dtype=jnp.float32) / (DK // 2 - 1))
    angles = positions[:, None] * frequency[None, :]
    normed = low(layer_norm(tokens, norm_gain, 1e-05))
    query_raw = low_back(matmul(normed, w_query)).reshape(TOKENS, H, DK)
    key_raw = low_back(matmul(normed, w_key)).reshape(TOKENS, H, DK)
    value_rows = low(low_back(matmul(normed, w_value))).reshape(TOKENS, H, DV)
    gate_raw = low_back(matmul(normed, w_gate))
    queries = low(rotate(query_raw, angles))
    key_rows = low(rotate(key_raw, angles) / math.sqrt(DK))
    retained = low_back(retention(queries, key_rows, value_rows))
    grouped = layer_norm(retained, 1.0, 0.5).reshape(TOKENS, H * DV) * group_gain
    mixed_out = low(jax.nn.silu(gate_raw) * grouped)
    residual = tokens + low_back(matmul(mixed_out, w_output))
    normed_two = low(layer_norm(residual, mlp_gain, 1e-05))
    up_one = low_back(matmul(normed_two, w_first))
    up_two = low_back(matmul(normed_two, w_second))
    hidden = low(gelu_exact(up_one) * up_two)
    return residual + matmul(hidden, w_third)

def reference(tokens, norm_gain, w_query, w_key, w_value, w_gate, group_gain, w_output, mlp_gain, w_first, w_second, w_third, cotangent):
    primal = (tokens.astype(jnp.float32), norm_gain.astype(jnp.float32), w_query.astype(jnp.float32), w_key.astype(jnp.float32), w_value.astype(jnp.float32), w_gate.astype(jnp.float32), group_gain.astype(jnp.float32), w_output.astype(jnp.float32), mlp_gain.astype(jnp.float32), w_first.astype(jnp.float32), w_second.astype(jnp.float32), w_third.astype(jnp.float32))
    output, pullback = jax.vjp(forward, *primal)
    gradients = pullback(cotangent.astype(jnp.float32))
    return (output.astype(jnp.bfloat16), gradients[0].astype(jnp.bfloat16), gradients[1], gradients[2], gradients[3], gradients[4], gradients[5], gradients[6], gradients[7], gradients[8], gradients[9], gradients[10], gradients[11])
```

```python
import functools
import math

import jax
import jax.numpy as jnp
from jax import lax
from jax.experimental import pallas as pl
from jax.experimental.pallas import tpu as pltpu
from jax.sharding import PartitionSpec as P

DK = 256
DV = 432
DVP = 512
BLK = 512
F32 = jnp.float32
BF16 = jnp.bfloat16


def contract(left_side, right_side, left_dim, right_dim):
    return lax.dot_general(
        left_side,
        right_side,
        (((left_dim,), (right_dim,)), ((), ())),
        preferred_element_type=F32,
    )


def row_stats(values, epsilon):
    centred = values - jnp.mean(values, axis=-1, keepdims=True)
    inverse = lax.rsqrt(jnp.mean(centred * centred, axis=-1, keepdims=True) + epsilon)
    return (centred * inverse, inverse)


def gelu_parts(values):
    cumulative = 0.5 * (1.0 + jax.scipy.special.erf(values / math.sqrt(2.0)))
    density = jnp.exp(-0.5 * values * values) / math.sqrt(2.0 * math.pi)
    return (values * cumulative, cumulative + values * density)


def head_reduce_scatter(terms):
    return lax.psum_scatter(terms.astype(BF16), "head", scatter_dimension=1, tiled=True).astype(F32)


def head_allreduce(terms):
    return lax.psum(terms.astype(BF16), "head").astype(F32)


def seq_carry(state, factor, reverse):
    n, me = lax.axis_size("seq"), lax.axis_index("seq")
    pieces = lax.all_gather(state.astype(BF16), "seq")
    total = jnp.zeros_like(state)
    for k in range(n):
        at = n - 1 - k if reverse else k
        longer = factor[:, None, None] * total + pieces[at].astype(F32)
        total = jnp.where((at > me) if reverse else (at < me), longer, total)
    return total


CHUNK = 16
PACE = 3
PIECE = 32
PIECES = -(-DV // PIECE)
LAG = 2
MESH = pl.DeviceIdType.MESH


def chain_kernel(
    n,
    small_h, hid_h, cot_h, mixed_h, branch_h, d1_h, d2_h, d1_far_h, d2_far_h, mid_h, mid_far_h, near_h, far_h,
    in_h, in_far_h,
    full_ref,
    g_ref, land_ref, cross_ref, wide_a, wide_b, slab_a, slab_b, give, take,
    load_sem, give_sem, take_sem, cross_sem, cross_sent, recv_sem, back_sem, send_sem, far_sem, side_sem, near_sem, own_sem,
):
    s = lax.axis_index("seq")
    z, x = s // 2, s % 2
    partner = s + 1 - 2 * x
    T, D = mid_h.shape

    def half(i):
        return pl.ds(pl.multiple_of(i * DVP, 128), DVP)

    def load(k, src, dst):
        return pltpu.make_async_copy(src, dst, load_sem.at[k])

    small = pl.ds(7 * DV + 2 * DK, 16)
    whole = 2 * DV // CHUNK
    loads_third = [
        load(0, hid_h, slab_a.at[0]), load(1, cot_h, wide_a.at[0]), load(14, small_h, g_ref.at[small]),
    ]
    loads_out = [load(2, mixed_h, slab_b.at[0, :, pl.ds(0, 2 * DVP)]), load(3, branch_h, wide_b)]
    loads_mid = [
        load(4, d1_h.at[:, half(x)], slab_a.at[0, :, pl.ds(0, DVP)]),
        load(5, d2_h.at[:, half(x)], slab_a.at[0, :, pl.ds(DVP, DVP)]),
        load(6, d1_far_h, slab_a.at[1, :, pl.ds(0, DVP)]),
        load(7, d2_far_h, slab_a.at[1, :, pl.ds(DVP, DVP)]),
        load(8, mid_h, wide_a.at[0]), load(9, mid_far_h, wide_a.at[1]),
    ]
    loads_in = [
        load(10, near_h, slab_b.at[0]), load(11, far_h, slab_b.at[1]), load(12, in_h, wide_a.at[0]),
        load(13, in_far_h, wide_a.at[1]),
    ]
    for copy in loads_third + loads_out:
        copy.start()
    spare = 2 * n * CHUNK - small.start - small.size
    if spare:
        g_ref[pl.ds(small.start + small.size, spare), :] = jnp.zeros((spare, D), BF16)

    greet((), partner)

    def chunk(j):
        return pl.ds(pl.multiple_of(j * CHUNK, 16), CHUNK)

    def remote(src, dst, send, recv, to):
        return pltpu.make_async_remote_copy(
            src_ref=src, dst_ref=dst, send_sem=send, recv_sem=recv,
            device_id={"seq": to}, device_id_type=MESH,
        )

    def pump(t):
        for flow in range(2):
            p = z if flow == 0 else 3 - z
            ahead = s + 2 if flow == 0 else s - 2
            behind = s - 2 if flow == 0 else s + 2
            i = t - LAG * p
            j = 2 * i + flow
            live = (i >= 0) & (i < n)

            @pl.when(live & (p == 0))
            def _():
                remote(g_ref.at[chunk(j)], land_ref.at[chunk(j)], send_sem.at[flow],
                       recv_sem.at[j], ahead).start()

            @pl.when(live & (p > 0))
            def _():
                pltpu.make_async_copy(land_ref.at[chunk(j)], land_ref.at[chunk(j)], recv_sem.at[j]).wait()
                land_ref[chunk(j), :] = (
                    land_ref[chunk(j), :].astype(F32) + g_ref[chunk(j), :].astype(F32)
                ).astype(BF16)

            @pl.when(live & (p > 0) & (p < 3))
            def _():
                remote(land_ref.at[chunk(j)], land_ref.at[chunk(j)], send_sem.at[flow],
                       recv_sem.at[j], ahead).start()

            @pl.when(live & (p == 3) & (j >= whole))
            def _():
                remote(land_ref.at[chunk(j)], full_ref.at[x, chunk(j)], far_sem.at[flow],
                       back_sem.at[j], behind).start()
                remote(land_ref.at[chunk(j)], full_ref.at[x, chunk(j)], side_sem.at[flow],
                       near_sem, partner).start()
                pltpu.make_async_copy(
                    land_ref.at[chunk(j)], full_ref.at[x, chunk(j)], own_sem
                ).start()

            @pl.when(live & (p == 3) & (j < whole))
            def _():
                remote(land_ref.at[chunk(j)], cross_ref.at[chunk(i)], cross_sent, cross_sem.at[i], partner).start()

            i1 = i - 1
            j1 = 2 * i1 + flow

            @pl.when((i1 >= 0) & (p == 3) & (j1 < whole))
            def _():
                here = cross_ref.at[chunk(i1)]
                pltpu.make_async_copy(here, here, cross_sem.at[i1]).wait()
                cross_ref[chunk(i1), :] = (
                    cross_ref[chunk(i1), :].astype(F32) + land_ref[chunk(j1), :].astype(F32)
                ).astype(BF16)
                remote(here, full_ref.at[x, chunk(j1)], far_sem.at[flow], back_sem.at[j1], behind).start()
                pltpu.make_async_copy(here, full_ref.at[x, chunk(j1)], own_sem).start()

            i2 = t - 6 * LAG - 1 + LAG * p
            j2 = 2 * i2 + flow
            live2 = (i2 >= 0) & (i2 < n) & (p < 3)

            @pl.when(live2)
            def _():
                pltpu.make_async_copy(
                    land_ref.at[chunk(j2)], full_ref.at[x, chunk(j2)], back_sem.at[j2]
                ).wait()

            @pl.when(live2 & (j2 >= whole))
            def _():
                remote(full_ref.at[x, chunk(j2)], full_ref.at[x, chunk(j2)], side_sem.at[flow],
                       near_sem, partner).start()

            @pl.when(live2 & (p > 0))
            def _():
                remote(full_ref.at[x, chunk(j2)], full_ref.at[x, chunk(j2)], far_sem.at[flow],
                       back_sem.at[j2], behind).start()

    def unit(u):
        return pl.ds(pl.multiple_of(DV * (u // 4) + 128 * (u % 4), 16), 128)

    def columns(k):
        return pl.ds(pl.multiple_of(k * 128, 128), 128)

    def block(u):
        return pl.ds(pl.multiple_of(u * 128, 128), 128)

    def piece(k):
        return pl.ds(pl.multiple_of(k * PIECE, 32), PIECE)

    def trade(k):
        return remote(give.at[piece(k)], take.at[piece(k)], give_sem.at[k], take_sem.at[k], partner)

    def taken(u, size):
        for k in range(size // PIECE if size == 128 else 2):
            here = take.at[piece(4 * u + k)]
            pltpu.make_async_copy(here, here, take_sem.at[4 * u + k]).wait()
        mine = pl.ds(pl.multiple_of(4 * DV + 128 * u, 16), size)
        theirs = pl.ds(pl.multiple_of(u * 128, 128), size)
        g_ref[mine, :] = (g_ref[mine, :].astype(F32) + take[theirs, :].astype(F32)).astype(BF16)

    def both(slab, wide, k):
        near = contract(slab[0, :, columns(k)], wide[0], 0, 0)
        return (near + contract(slab[1, :, columns(k)], wide[1], 0, 0)).astype(BF16)

    def alone(k, wide):
        return contract(k, wide, 0, 0).astype(BF16)

    for copy in loads_third:
        copy.wait()
    g_ref[unit(0), :] = alone(slab_a[0, :, columns(0)], wide_a[0])

    def step(t, carry):
        tick = t // PACE
        beat = t % PACE == 0
        u = tick - 14

        @pl.when(beat & (u >= 0) & (u < 3))
        def _():
            taken(u, 128)

        @pl.when(beat & (u == 3))
        def _():
            taken(3, DV - 384)

        pump(t)

        @pl.when(beat & (tick == 0))
        def _():
            for copy in loads_out:
                copy.wait()

        @pl.when(beat & (tick < 6))
        def _():
            g_ref[unit(1 + tick), :] = alone(slab_a[0, :, columns(1 + tick)], wide_a[0])

        @pl.when(beat & (tick == 6))
        def _():
            last = alone(slab_a[0, :, columns(7)], wide_a[0])
            g_ref[pl.ds(DV + 384, DV - 384), :] = last[: DV - 384]

        @pl.when(beat & (tick < 4))
        def _():
            give[block(tick), :] = alone(slab_b[0, :, columns((1 - x) * 4 + tick)], wide_b[...])
            g_ref[unit(16 + tick), :] = alone(slab_b[0, :, columns(x * 4 + tick)], wide_b[...])

        k = (t - 4 * PACE) // 2

        @pl.when((k >= 0) & (k < PIECES) & (t % 2 == 0))
        def _():
            trade(k).start()

        @pl.when(beat & (tick == 6))
        def _():
            for copy in loads_mid:
                copy.start()

        @pl.when(beat & (tick == 7))
        def _():
            for copy in loads_mid:
                copy.wait()

        @pl.when(beat & (tick >= 7) & (tick < 14))
        def _():
            g_ref[unit(1 + tick), :] = both(slab_a, wide_a, tick - 7)

        @pl.when(beat & (tick == 14))
        def _():
            g_ref[pl.ds(3 * DV + 384, DV - 384), :] = both(slab_a, wide_a, 7)[: DV - 384]

        @pl.when(beat & (tick == 15))
        def _():
            for copy in loads_in:
                copy.start()

        @pl.when(beat & (tick == 17))
        def _():
            for copy in loads_in:
                copy.wait()

        @pl.when(beat & (tick >= 17) & (tick < 29))
        def _():
            g_ref[unit(3 + tick), :] = both(slab_b, wide_a, tick - 17)

        return carry

    lax.fori_loop(0, n + 6 * LAG + 1, step, 0)

    for k in range(PIECES):
        trade(k).wait_send()
    for flow in range(2):
        p = z if flow == 0 else 3 - z
        mine = (whole + 1 - flow) // 2

        def drain(sem, count):
            part = land_ref.at[pl.ds(0, count * CHUNK)]
            pltpu.make_async_copy(part, part, sem).wait()

        @pl.when(p < 3)
        def _():
            drain(send_sem.at[flow], n)

        @pl.when(p > 0)
        def _():
            drain(far_sem.at[flow], n)

        @pl.when(p == 3)
        def _():
            drain(own_sem, n)
            drain(cross_sent, mine)

        drain(side_sem.at[flow], n - mine)
    got = full_ref.at[1 - x, pl.ds(whole * CHUNK, (2 * n - whole) * CHUNK)]
    pltpu.make_async_copy(got, got, near_sem).wait()


def chain_sum(
    small, hidden, cot, mixed, grad_branch, d1, d2, far_d1, far_d2, mid, far_mid, near, far, normed, far_normed
):
    T, D = mid.shape
    unit = 2 * CHUNK
    total = -(-(7 * DV + 2 * DK + 16) // unit) * unit
    chunks = total // CHUNK
    dma = pltpu.SemaphoreType.DMA
    return pl.pallas_call(
        functools.partial(chain_kernel, chunks // 2),
        out_shape=jax.ShapeDtypeStruct((2, total, D), BF16),
        in_specs=[pl.BlockSpec(memory_space=pl.ANY)] * 15,
        out_specs=pl.BlockSpec(memory_space=pl.ANY),
        scratch_shapes=[
            pltpu.VMEM((total, D), BF16), pltpu.VMEM((total, D), BF16), pltpu.VMEM((-(-DV // unit) * unit, D), BF16),
            pltpu.VMEM((2, T, D), BF16), pltpu.VMEM((T, D), BF16),
            pltpu.VMEM((2, T, 2 * DVP), BF16), pltpu.VMEM((2, T, 2 * DVP + 2 * DK), BF16),
            pltpu.VMEM((DVP, D), BF16), pltpu.VMEM((DVP, D), BF16),
            dma((15,)), dma((PIECES,)), dma((PIECES,)), dma((DV // CHUNK + 1,)), dma, dma((chunks,)), dma((chunks,)), dma((2,)), dma((2,)), dma((2,)),
            dma, dma,
        ],
        compiler_params=pltpu.CompilerParams(
            collective_id=0, has_side_effects=True, vmem_limit_bytes=63 * 2**20
        ),
        name="gradient_chains",
    )(
        small, hidden, cot, mixed, grad_branch, d1, d2, far_d1, far_d2, mid, far_mid, near, far, normed, far_normed,
    )


def finish_kernel(layout, full_ref, small_ref, whole_ref, *outs):
    row = layout[-1][0] + layout[-1][1]
    small_ref[...] = full_ref[0, row : row + 8, :].astype(F32) + full_ref[1, row : row + 8, :].astype(F32)
    x = lax.axis_index("seq") % 2
    whole = whole_ref.shape[0]
    whole_ref[...] = jnp.where(x == 0, full_ref[0, :whole, :], full_ref[1, :whole, :]).astype(F32)
    for (at, size, flip), out_ref in zip(layout, outs):
        for i in range(2):
            part = full_ref[i, at : at + size, :].astype(F32)
            if flip:
                out_ref[:, i * size : (i + 1) * size] = part.T
            else:
                out_ref[i * size : (i + 1) * size, :] = part


def finish(full, layout):
    D, tile = full.shape[2], 256
    lead = layout[0][0]
    specs = [pl.BlockSpec((8, tile), lambda i: (0, i)), pl.BlockSpec((lead, tile), lambda i: (0, i))]
    shapes = [jax.ShapeDtypeStruct((8, D), F32), jax.ShapeDtypeStruct((lead, D), F32)]
    for _, size, flip in layout:
        shapes.append(jax.ShapeDtypeStruct((D, 2 * size) if flip else (2 * size, D), F32))
        specs.append(
            pl.BlockSpec((tile, 2 * size), lambda i: (i, 0))
            if flip
            else pl.BlockSpec((2 * size, tile), lambda i: (0, i))
        )
    return pl.pallas_call(
        functools.partial(finish_kernel, layout),
        grid=(D // tile,),
        in_specs=[pl.BlockSpec((2, full.shape[1], tile), lambda i: (0, 0, i))],
        out_specs=specs,
        out_shape=shapes,
        compiler_params=pltpu.CompilerParams(vmem_limit_bytes=56 * 2**20),
        name="gradients_to_float32",
    )(full)


def offsets():
    return lax.broadcasted_iota(jnp.int32, (BLK, 1), 0).astype(F32)


def decay_row(logc, width, exponent):
    return jnp.exp(jnp.full((1, width), exponent, F32) * logc)


def decay_square(logc):
    row = lax.broadcasted_iota(jnp.int32, (BLK, BLK), 0)
    col = lax.broadcasted_iota(jnp.int32, (BLK, BLK), 1)
    lag = (row - col).astype(F32)
    return jnp.where(lag >= 0, jnp.exp(jnp.maximum(lag, 0.0) * logc), 0.0)


def turn(values, cosine, sine):
    a, b = values[:, : DK // 2], values[:, DK // 2 :]
    return jnp.concatenate([a * cosine - b * sine, b * cosine + a * sine], axis=1)


def rows(b):
    return pl.ds(b * BLK, BLK)


def fwd_state_kernel(nb, logc_ref, q_ref, k_ref, v_ref, cos_ref, sin_ref, qo_ref, ko_ref, s_ref):
    logc = logc_ref[pl.program_id(0)]
    o = offsets()
    to_end = jnp.exp((BLK - 1.0 - o) * logc)
    across = decay_row(logc, DVP, float(BLK))
    state = None
    for b in range(nb):
        cosine, sine = cos_ref[rows(b), :], sin_ref[rows(b), :]
        qo_ref[rows(b), :] = turn(q_ref[rows(b), :], cosine, sine).astype(BF16)
        key = (turn(k_ref[rows(b), :], cosine, sine) * (1.0 / math.sqrt(DK))).astype(BF16)
        ko_ref[rows(b), :] = key
        scaled = (key.astype(F32) * to_end).astype(BF16)
        new = contract(scaled, v_ref[rows(b), :], 0, 0)
        state = new if state is None else across * state + new
        s_ref[b] = state


def total_state(b, logc, s_in, s_ref):
    carried = s_in if b == 0 else decay_row(logc, DVP, float(b * BLK)) * s_in
    return carried if b == 0 else carried + s_ref[b - 1]


def group_stats(retained):
    real = lax.broadcasted_iota(jnp.int32, retained.shape, 1) < DV
    mean = jnp.sum(retained, axis=1, keepdims=True) * (1.0 / DV)
    centred = jnp.where(real, retained - mean, 0.0)
    var = jnp.sum(centred * centred, axis=1, keepdims=True) * (1.0 / DV)
    inverse = lax.rsqrt(var + 0.5)
    return centred * inverse, inverse


def fwd_out_kernel(
    nb, logc_ref, q_ref, k_ref, v_ref, s_ref, in_ref, gate_ref, gain_ref, mixed_ref, ret_ref
):
    logc = logc_ref[pl.program_id(0)]
    mask = decay_square(logc)
    into = jnp.exp((offsets() + 1.0) * logc)
    s_in = in_ref[...]
    for b in range(nb):
        query = q_ref[rows(b), :]
        scores = contract(query, k_ref[rows(b), :], 1, 1)
        weights = (scores * mask).astype(BF16)
        state = total_state(b, logc, s_in, s_ref).astype(BF16)
        scaled = (query.astype(F32) * into).astype(BF16)
        retained = contract(weights, v_ref[rows(b), :], 1, 0) + contract(scaled, state, 1, 0)
        ret_ref[rows(b), :] = retained
        ohat, _ = group_stats(retained)
        gate = gate_ref[rows(b), :]
        act = gate * jax.nn.sigmoid(gate)
        mixed_ref[rows(b), :] = (act * (ohat * gain_ref[...])).astype(BF16)


def bwd_mix_kernel(
    nb, logc_ref, dm_ref, ret_ref, gate_ref, gain_ref, q_ref, dg_ref, dr_ref, gg_ref, ds_ref
):
    logc = logc_ref[pl.program_id(0)]
    into = jnp.exp((offsets() + 1.0) * logc)
    gain = gain_ref[...]
    total = jnp.zeros((1, DVP), F32)
    state = jnp.zeros((DK, DVP), F32)
    for b in range(nb):
        dmixed = dm_ref[rows(b), :]
        gate = gate_ref[rows(b), :]
        ohat, inverse = group_stats(ret_ref[rows(b), :])
        sig = jax.nn.sigmoid(gate)
        dgrouped = dmixed * (gate * sig)
        dg_ref[rows(b), :] = (
            dmixed * (ohat * gain) * sig * (1.0 + gate * (1.0 - sig))
        ).astype(BF16)
        total = total + jnp.sum(dgrouped * ohat, axis=0, keepdims=True)
        e = dgrouped * gain
        mean = jnp.sum(e, axis=1, keepdims=True) * (1.0 / DV)
        cross = jnp.sum(e * ohat, axis=1, keepdims=True) * (1.0 / DV)
        real = lax.broadcasted_iota(jnp.int32, e.shape, 1) < DV
        dret = jnp.where(real, inverse * (e - mean - ohat * cross), 0.0).astype(BF16)
        dr_ref[rows(b), :] = dret
        scaled = (q_ref[rows(b), :].astype(F32) * into).astype(BF16)
        new = contract(scaled, dret, 0, 0)
        state = state + (new if b == 0 else decay_row(logc, DVP, float(b * BLK)) * new)
    gg_ref[...] = total
    ds_ref[...] = state


def bwd_ret_kernel(
    nb, logc_ref, q_ref, k_ref, v_ref, dr_ref, s_ref, in_ref, out_ref, cos_ref, sin_ref,
    dq_ref, dk_ref, dv_ref,
):
    logc = logc_ref[pl.program_id(0)]
    mask = decay_square(logc)
    o = offsets()
    into = jnp.exp((o + 1.0) * logc)
    to_end = jnp.exp((BLK - 1.0 - o) * logc)
    across = decay_row(logc, DVP, float(BLK))
    s_in = in_ref[...]
    later = out_ref[...]
    for b in reversed(range(nb)):
        query, key = q_ref[rows(b), :], k_ref[rows(b), :]
        value, dret = v_ref[rows(b), :], dr_ref[rows(b), :]
        weights = (contract(query, key, 1, 1) * mask).astype(BF16)
        dweights = (contract(dret, value, 1, 1) * mask).astype(BF16)
        state = total_state(b, logc, s_in, s_ref).astype(BF16)
        low = later.astype(BF16)
        dquery = contract(dweights, key, 1, 0) + contract(dret, state, 1, 1) * into
        dkey = contract(dweights, query, 0, 0) + contract(value, low, 1, 1) * to_end
        scaled = (key.astype(F32) * to_end).astype(BF16)
        dvalue = contract(weights, dret, 0, 0) + contract(scaled, low, 1, 0)
        cosine, sine = cos_ref[rows(b), :], sin_ref[rows(b), :]
        dq_ref[rows(b), :] = turn(dquery, cosine, -sine).astype(BF16)
        dk_ref[rows(b), :] = (turn(dkey, cosine, -sine) * (1.0 / math.sqrt(DK))).astype(BF16)
        dv_ref[rows(b), :] = dvalue.astype(BF16)
        if b > 0:
            qs = (query.astype(F32) * into).astype(BF16)
            later = across * later + contract(qs, dret, 0, 0)


def per_head(kernel, heads, T, ins, outs, name):
    nb = T // BLK

    def spec(kind):
        if kind == "smem":
            return pl.BlockSpec(memory_space=pltpu.SMEM)
        if kind == "rot":
            return pl.BlockSpec((T, DK // 2), lambda h: (0, 0))
        if kind == "key":
            return pl.BlockSpec((T, DK), lambda h: (0, h))
        if kind == "val":
            return pl.BlockSpec((T, DVP), lambda h: (0, h))
        if kind == "gain":
            return pl.BlockSpec((1, DVP), lambda h: (0, h))
        if kind == "state":
            return pl.BlockSpec((None, DK, DVP), lambda h: (h, 0, 0))
        if kind == "states":
            return pl.BlockSpec((nb, None, DK, DVP), lambda h: (0, h, 0, 0))
        raise ValueError(kind)

    def shape(kind, dtype):
        full = {
            "key": (T, heads * DK),
            "val": (T, heads * DVP),
            "gain": (1, heads * DVP),
            "state": (heads, DK, DVP),
            "states": (nb, heads, DK, DVP),
        }[kind]
        return jax.ShapeDtypeStruct(full, dtype)

    return pl.pallas_call(
        functools.partial(kernel, nb),
        grid=(heads,),
        in_specs=[spec(kind) for kind in ins],
        out_specs=[spec(kind) for kind, _ in outs],
        out_shape=[shape(kind, dtype) for kind, dtype in outs],
        compiler_params=pltpu.CompilerParams(vmem_limit_bytes=48 * 2**20),
        name=name,
    )


ROWS = 128


def own_block(value):
    h = lax.axis_index("head")
    y, c = h // 2, h % 2
    cols = value.shape[1] // 4
    part = [value[:, i * cols : (i + 1) * cols] for i in range(4)]
    return jnp.where(y == 0, jnp.where(c == 0, part[0], part[1]), jnp.where(c == 0, part[2], part[3]))


def reduce_scatter(scratch):
    keep, give, near, far, give_sem, near_sem, far_sent, far_sem = scratch
    h = lax.axis_index("head")
    y, c = h // 2, h % 2
    sibling, across = h + 1 - 2 * c, h + 2 - 4 * y
    cols = far.shape[1]

    def at(r):
        return pl.ds(pl.multiple_of(r * ROWS, ROWS), ROWS)

    def remote(src, dst, sent, got, to):
        return pltpu.make_async_remote_copy(
            src_ref=src, dst_ref=dst, send_sem=sent, recv_sem=got,
            device_id={"head": to}, device_id_type=MESH,
        )

    def to_sibling(r):
        slot = lax.rem(r, 2)
        return remote(give.at[slot], near.at[at(r)], give_sem.at[slot], near_sem.at[r], sibling)

    def spread(r, terms):
        slot = lax.rem(r, 2)

        @pl.when(r >= 2)
        def _():
            to_sibling(r).wait_send()

        part = [terms[:, i * cols : (i + 1) * cols] for i in range(4)]
        for i in range(2):
            place = slice(i * cols, (i + 1) * cols)
            keep[slot, :, place] = jnp.where(c == 0, part[2 * i], part[2 * i + 1])
            give[slot, :, place] = jnp.where(c == 0, part[2 * i + 1], part[2 * i]).astype(BF16)
        to_sibling(r).start()

    def collect(r):
        slot = lax.rem(r, 2)
        pltpu.make_async_copy(near.at[at(r)], near.at[at(r)], near_sem.at[r]).wait()
        chip = (keep[slot] + near[at(r), :].astype(F32)).astype(BF16)
        first, last = chip[:, :cols], chip[:, cols:]
        near[at(r), :cols] = jnp.where(y == 0, last, first)
        near[at(r), cols:] = jnp.where(y == 0, first, last)

    def pass_on(r):
        remote(near.at[at(r), pl.ds(0, cols)], far.at[at(r)], far_sent, far_sem.at[r], across).start()

    def gather(r):
        pltpu.make_async_copy(far.at[at(r)], far.at[at(r)], far_sem.at[r]).wait()
        return near[at(r), cols:].astype(F32) + far[at(r), :].astype(F32)

    def drain_near():
        for slot in range(2):
            to_sibling(slot).wait_send()

    def drain():
        drain_near()
        pltpu.make_async_copy(far, far, far_sent).wait()

    return spread, collect, pass_on, gather, drain_near, drain


def scatter_scratch(T, D):
    dma, nr = pltpu.SemaphoreType.DMA, T // ROWS
    return [
        pltpu.VMEM((2, ROWS, D // 2), F32), pltpu.VMEM((2, ROWS, D // 2), BF16),
        pltpu.VMEM((T, D // 2), BF16), pltpu.VMEM((T, D // 4), BF16),
        dma((2,)), dma((nr,)), dma, dma((nr,)),
    ]


def middle_general(mixed, all_tokens, all_cot, wo, w1, w2, w3, gain, heads):
    wo, w1, w2, w3 = [pad_rows(w, heads) for w in (wo, w1, w2, w3)]
    cols = all_tokens.shape[1] // lax.axis_size("head")
    own = lax.axis_index("head") * cols
    resid = all_tokens.astype(F32) + head_allreduce(jnp.dot(mixed, wo, preferred_element_type=F32))
    normal, inverse = row_stats(resid, 1e-05)
    normed = (normal * gain).astype(BF16)
    up_one, up_two = contract(normed, w1, 1, 1), contract(normed, w2, 1, 1)
    gelu_one, gelu_slope = gelu_parts(up_one)
    hidden = (gelu_one * up_two).astype(BF16)
    own_resid = lax.dynamic_slice_in_dim(resid, own, cols, axis=1)
    mlp_terms = jnp.dot(hidden, w3, preferred_element_type=F32)
    output = own_resid + head_reduce_scatter(mlp_terms)
    grad_hidden = contract(all_cot, w3, 1, 1)
    grad_one = (grad_hidden * up_two * gelu_slope).astype(BF16)
    grad_two = (grad_hidden * gelu_one).astype(BF16)
    grad = head_allreduce(
        jnp.dot(grad_one, w1, preferred_element_type=F32)
        + jnp.dot(grad_two, w2, preferred_element_type=F32)
    )
    gain_grad = jnp.sum(grad * normal, axis=0, keepdims=True)
    e = grad * gain
    resid_grad = all_cot.astype(F32) + inverse * (
        e
        - jnp.mean(e, axis=-1, keepdims=True)
        - normal * jnp.mean(e * normal, axis=-1, keepdims=True)
    )
    return (
        normed, hidden, grad_one, grad_two, output, None, resid_grad.astype(BF16),
        lax.dynamic_slice_in_dim(resid_grad, own, cols, axis=1),
        None,
        None,
        None,
        gain_grad,
    )


def middle_body(
    nr,
    parts,
    mixed_h, tok_h, cot_h, wo_h, w1_h, w2_h, w3_h, gain_ref,
    n2_h, hid_h, d1_h, d2_h, res_h, chip_h, db_h, dr_h, far2_h, far_d1_h, far_d2_h, mg_ref,
    mixed, tok, cot, wo, w1, w2, w3,
    keep, give, near, far, tot,
    s_n2, s_hid, s_d1, s_d2, s_res, s_db, s_dr,
    load_sem, mixed_sem, share_sem, shared_sem, hand_sem, acts_sem, give_sem, near_sem, far_sent, far_sem, tot_sent, tot_sem, out_sem,
    *scatter,
):
    h = lax.axis_index("head")
    y, c = h // 2, h % 2
    sibling, across = h + 1 - 2 * c, h + 2 - 4 * y
    D = tok.shape[1]
    half, cols = D // 2, D // 4

    s = lax.axis_index("seq")
    x = lax.rem(s, 2)
    partner = s + 1 - 2 * x
    U = w1.shape[0]
    real, room = w1_h.shape[0] // parts, U // parts
    loads = [
        pltpu.make_async_copy(tok_h, tok, load_sem.at[0]),
        pltpu.make_async_copy(cot_h, cot, load_sem.at[1]),
    ]
    weights = []
    for k, (src, dst) in enumerate([(wo_h, wo), (w1_h, w1), (w2_h, w2), (w3_h, w3)]):
        weights.append([
            pltpu.make_async_copy(
                src.at[pl.ds(i * real, real)], dst.at[pl.ds(i * room, real)], load_sem.at[2 + k * parts + i]
            )
            for i in range(parts)
        ])
    def at(r):
        return pl.ds(pl.multiple_of(r * ROWS, ROWS), ROWS)

    def fetch(r):
        slot = lax.rem(r, 2)
        return pltpu.make_async_copy(mixed_h.at[at(r)], mixed.at[slot], mixed_sem.at[slot])

    fetch(0).start()
    for load in weights[0]:
        load.start()
    fetch(1).start()
    for load in loads + weights[1] + weights[2] + weights[3]:
        load.start()
    for dst in (wo, w1, w2, w3):
        for i in range(parts):
            dst[i * room + real : (i + 1) * room, :] = jnp.zeros((room - real, D), BF16)
    barrier = pltpu.get_barrier_semaphore()
    for other in (sibling, across):
        pl.semaphore_signal(barrier, inc=1, device_id={"head": other}, device_id_type=MESH)
    pl.semaphore_signal(barrier, inc=1, device_id={"seq": partner}, device_id_type=MESH)
    pl.semaphore_wait(barrier, 3)
    mg_ref[...] = jnp.zeros_like(mg_ref)

    mine = pl.ds(pl.multiple_of(c * half, 128), half)
    theirs = pl.ds(pl.multiple_of((1 - x) * room, 128), room)

    def share(k, r):
        slot = lax.rem(r, 2)
        if k == 0:
            src, dst, got = s_n2.at[slot, :, mine], far2_h.at[at(r), mine], share_sem.at[r]
        else:
            stage, far_h = ((s_d1, far_d1_h), (s_d2, far_d2_h))[k - 1]
            src, dst, got = stage.at[slot, :, theirs], far_h.at[at(r)], acts_sem.at[k - 1]
        return pltpu.make_async_remote_copy(
            src_ref=src, dst_ref=dst, send_sem=shared_sem.at[k, slot], recv_sem=got,
            device_id={"seq": partner}, device_id_type=MESH,
        )

    def hand(r):
        here = far2_h.at[at(r), mine]
        return pltpu.make_async_remote_copy(
            src_ref=here, dst_ref=here, send_sem=hand_sem.at[0], recv_sem=hand_sem.at[1],
            device_id={"head": sibling}, device_id_type=MESH,
        )

    for load in weights[0]:
        load.wait()

    def remote(src, dst, sent, got, to):
        return pltpu.make_async_remote_copy(
            src_ref=src, dst_ref=dst, send_sem=sent, recv_sem=got,
            device_id={"head": to}, device_id_type=MESH,
        )

    def first(a, r, terms):
        slot = lax.rem(r, 2)

        @pl.when(r >= 2)
        def _():
            pltpu.make_async_copy(give.at[a, slot], give.at[a, slot], give_sem.at[a, slot]).wait()

        lo, hi = terms[:, :half], terms[:, half:]
        keep[a] = jnp.where(c == 0, lo, hi)
        give[a, slot] = jnp.where(c == 0, hi, lo).astype(BF16)
        remote(give.at[a, slot], near.at[a, at(r)], give_sem.at[a, slot], near_sem.at[a, r], sibling).start()

    def second(a, r):
        here = near.at[a, at(r)]
        pltpu.make_async_copy(here, here, near_sem.at[a, r]).wait()
        near[a, at(r)] = (keep[a] + near[a, at(r)].astype(F32)).astype(BF16)
        remote(here, far.at[a, at(r)], far_sent.at[a], far_sem.at[a, r], across).start()

    def third(a, r):
        here = far.at[a, at(r)]
        pltpu.make_async_copy(here, here, far_sem.at[a, r]).wait()
        tot[a, c, at(r)] = (near[a, at(r)].astype(F32) + far[a, at(r)].astype(F32)).astype(BF16)
        here = tot.at[a, c, at(r)]
        remote(here, here, tot_sent.at[a], tot_sem.at[a, r], sibling).start()

    def joined(a, r):
        return jnp.concatenate([tot[a, 0, at(r)], tot[a, 1, at(r)]], axis=1).astype(F32)

    def arrive(a, r):
        here = tot.at[a, 1 - c, at(r)]
        pltpu.make_async_copy(here, here, tot_sem.at[a, r]).wait()

    def put(k, r, stage, dst, value, shared=None):
        slot = lax.rem(r, 2)
        copy = pltpu.make_async_copy(stage.at[slot], dst.at[at(r)], out_sem.at[k, slot])

        @pl.when(r >= 2)
        def _():
            copy.wait()
            if shared is not None:
                share(shared, r).wait_send()

        stage[slot] = value
        copy.start()
        if shared is not None:
            share(shared, r).start()

    spread, collect, _, _, drain_near, _ = reduce_scatter(scatter)

    def step(t, carry):
        for a, late in ((0, 1), (1, 4)):
            r = t - late

            @pl.when((r >= 0) & (r < nr))
            def _():
                second(a, r)

        r = t - 4

        @pl.when((r >= 0) & (r < nr))
        def _():
            collect(r)

        for a, late in ((0, 2), (1, 5)):
            r = t - late

            @pl.when((r >= 0) & (r < nr))
            def _():
                third(a, r)

        @pl.when(t < nr)
        def _():
            fetch(t).wait()
            first(0, t, jnp.dot(mixed[lax.rem(t, 2)], wo[...], preferred_element_type=F32))

        @pl.when(t + 2 < nr)
        def _():
            fetch(t + 2).start()

        r = t - 3

        @pl.when(r == 0)
        def _():
            for load in loads + weights[1] + weights[2] + weights[3]:
                load.wait()

        @pl.when((r >= 0) & (r < nr))
        def _():
            arrive(0, r)
            resid = tok[at(r), :].astype(F32) + joined(0, r)
            put(0, r, s_res, res_h, own_block(resid))
            normal, _ = row_stats(resid, 1e-05)
            normed = (normal * gain_ref[...]).astype(BF16)
            put(1, r, s_n2, n2_h, normed, 0)
            up_one, up_two = contract(normed, w1[...], 1, 1), contract(normed, w2[...], 1, 1)
            grad_hidden = contract(cot[at(r), :], w3[...], 1, 1)
            gelu_one, gelu_slope = gelu_parts(up_one)
            hidden = (gelu_one * up_two).astype(BF16)
            grad_one = (grad_hidden * up_two * gelu_slope).astype(BF16)
            grad_two = (grad_hidden * gelu_one).astype(BF16)
            terms = jnp.dot(grad_one, w1[...], preferred_element_type=F32)
            first(1, r, terms + jnp.dot(grad_two, w2[...], preferred_element_type=F32))
            put(2, r, s_hid, hid_h, hidden)
            put(3, r, s_d1, d1_h, grad_one, 1)
            put(4, r, s_d2, d2_h, grad_two, 2)
            spread(r, jnp.dot(hidden, w3[...], preferred_element_type=F32))

        g = t - 6

        @pl.when(g >= 0)
        def _():
            arrive(1, g)
            normal, inverse = row_stats(tok[at(g), :].astype(F32) + joined(0, g), 1e-05)
            grad = joined(1, g)
            mg_ref[...] += jnp.sum(grad * normal, axis=0, keepdims=True)
            e = grad * gain_ref[...]
            resid_grad = cot[at(g), :].astype(F32) + inverse * (
                e
                - jnp.mean(e, axis=-1, keepdims=True)
                - normal * jnp.mean(e * normal, axis=-1, keepdims=True)
            )
            put(5, g, s_db, db_h, resid_grad.astype(BF16))
            put(6, g, s_dr, dr_h, own_block(resid_grad))

        r = t - 5

        @pl.when((r >= 0) & (r < nr))
        def _():
            here = far2_h.at[at(r), mine]
            pltpu.make_async_copy(here, here, share_sem.at[r]).wait()
            hand(r).start()

        return carry

    lax.fori_loop(0, nr + 6, step, 0)

    other = far2_h.at[:, pl.ds(pl.multiple_of((1 - c) * half, 128), half)]
    pltpu.make_async_copy(other, other, hand_sem.at[0]).wait()
    pltpu.make_async_copy(other, other, hand_sem.at[1]).wait()
    for k in range(3):
        for slot in range(2):
            share(k, slot).wait_send()
    pltpu.make_async_copy(far_d1_h, far_d1_h, acts_sem.at[0]).wait()
    pltpu.make_async_copy(far_d2_h, far_d2_h, acts_sem.at[1]).wait()
    for a in range(2):
        for slot in range(2):
            pltpu.make_async_copy(give.at[a, slot], give.at[a, slot], give_sem.at[a, slot]).wait()
        pltpu.make_async_copy(far.at[a], far.at[a], far_sent.at[a]).wait()
        pltpu.make_async_copy(tot.at[a, 0], tot.at[a, 0], tot_sent.at[a]).wait()
    drain_near()
    chips = pltpu.make_async_copy(scatter[2], chip_h, scatter[6])
    chips.start()
    chips.wait()
    for k, stage in enumerate([s_res, s_n2, s_hid, s_d1, s_d2, s_db, s_dr]):
        for slot in range(2):
            pltpu.make_async_copy(stage.at[slot], stage.at[slot], out_sem.at[k, slot]).wait()


def middle_kernel(mixed, all_tokens, all_cot, wo, w1, w2, w3, gain, heads):
    T, D = all_tokens.shape
    U, half, cols, nr = mixed.shape[1], D // 2, D // 4, T // ROWS
    low, wide = functools.partial(jax.ShapeDtypeStruct, dtype=BF16), functools.partial(
        jax.ShapeDtypeStruct, dtype=F32
    )
    anywhere, vmem = pl.BlockSpec(memory_space=pl.ANY), pl.BlockSpec(memory_space=pltpu.VMEM)
    dma = pltpu.SemaphoreType.DMA
    macs = T * U * D * 7
    return pl.pallas_call(
        functools.partial(middle_body, nr, heads),
        out_shape=[
            low((T, D)), low((T, U)), low((T, U)), low((T, U)), wide((T, cols)), low((T, half)),
            low((T, D)), wide((T, cols)), low((T, D)), low((T, U // heads)), low((T, U // heads)),
            wide((1, D)),
        ],
        in_specs=[anywhere] * 7 + [vmem],
        out_specs=[anywhere] * 11 + [vmem],
        scratch_shapes=[
            pltpu.VMEM((2, ROWS, U), BF16), pltpu.VMEM((T, D), BF16), pltpu.VMEM((T, D), BF16),
            pltpu.VMEM((U, D), BF16), pltpu.VMEM((U, D), BF16), pltpu.VMEM((U, D), BF16),
            pltpu.VMEM((U, D), BF16),
            pltpu.VMEM((2, ROWS, half), F32), pltpu.VMEM((2, 2, ROWS, half), BF16),
            pltpu.VMEM((2, T, half), BF16), pltpu.VMEM((2, T, half), BF16),
            pltpu.VMEM((2, 2, T, half), BF16),
            pltpu.VMEM((2, ROWS, D), BF16), pltpu.VMEM((2, ROWS, U), BF16),
            pltpu.VMEM((2, ROWS, U), BF16), pltpu.VMEM((2, ROWS, U), BF16),
            pltpu.VMEM((2, ROWS, cols), F32), pltpu.VMEM((2, ROWS, D), BF16),
            pltpu.VMEM((2, ROWS, cols), F32),
            dma((2 + 4 * heads,)), dma((2,)), dma((nr,)), dma((3, 2)), dma((2,)), dma((2,)), dma((2, 2)), dma((2, nr)), dma((2,)), dma((2, nr)), dma((2,)), dma((2, nr)),
            dma((7, 2)),
        ] + scatter_scratch(T, D),
        compiler_params=pltpu.CompilerParams(
            collective_id=1, has_side_effects=True, vmem_limit_bytes=63 * 2**20
        ),
        cost_estimate=pl.CostEstimate(
            flops=2 * macs, bytes_accessed=50 * 2**20, transcendentals=2 * T * U
        ),
        name="mixed_to_dbranch",
    )(mixed, all_tokens, all_cot, wo, w1, w2, w3, gain)


def carry_state(reverse, logc_ref, T, own, total, bufs, sems):
    low, side, into, out = bufs
    low_sem, side_sem, into_sem, out_sem = sems
    s = lax.axis_index("seq")
    z, x = s // 2, s % 2
    partner = s + 1 - 2 * x
    p = 3 - z if reverse else z
    ahead = s - 2 if reverse else s + 2
    first = (x == 1) if reverse else (x == 0)
    parts = 4
    size = DK // parts

    def remote(src, dst, sent, got, to):
        return pltpu.make_async_remote_copy(
            src_ref=src, dst_ref=dst, send_sem=sent, recv_sem=got,
            device_id={"seq": to}, device_id_type=MESH,
        )

    def part(i):
        return pl.ds(i * size, size)

    def trade(k, i):
        head = 1 - x if k == 0 else x
        return remote(low.at[head, part(i)], side.at[head, part(i)], low_sem.at[k, i], side_sem.at[k, i], partner)

    def forward(head, k, i):
        return remote(out.at[head, part(i)], into.at[head, part(i)], out_sem.at[k, i], into_sem.at[k, i], ahead)

    def factor(h, width=DVP):
        return jnp.exp(jnp.full((1, width), float(T), F32) * logc_ref[h])

    def start():
        low[...] = own[...].astype(BF16)
        for k in range(2):
            for i in range(parts):
                trade(k, i).start()

    def finish():
        for k in range(2):
            head = x if k == 0 else 1 - x
            f = factor(head)
            for i in range(parts):
                here = side.at[head, part(i)]
                pltpu.make_async_copy(here, here, side_sem.at[k, i]).wait()
                mine, others = low[head, part(i)].astype(F32), side[head, part(i)].astype(F32)
                early = jnp.where(first, mine, others)
                pair = f * early + jnp.where(first, others, mine)

                @pl.when(p == 0)
                def _():
                    out[head, part(i)] = pair.astype(BF16)
                    into[head, part(i)] = jnp.zeros((size, DVP), BF16)

                @pl.when(p > 0)
                def _():
                    here = into.at[head, part(i)]
                    pltpu.make_async_copy(here, here, into_sem.at[k, i]).wait()
                    out[head, part(i)] = (pair + f * f * into[head, part(i)].astype(F32)).astype(BF16)

                @pl.when(p < 3)
                def _():
                    forward(head, k, i).start()

                before = into[head, part(i)].astype(F32)
                total[head, part(i)] = jnp.where(first, before, f * before + early)

        for k in range(2):
            for i in range(parts):
                trade(k, i).wait_send()

                @pl.when(p < 3)
                def _():
                    forward(x if k == 0 else 1 - x, k, i).wait_send()

    return start, finish


def carry_scratch():
    dma = pltpu.SemaphoreType.DMA
    state = pltpu.VMEM((2, DK, DVP), BF16)
    return [state] * 4 + [dma((2, 4))] * 4


def greet(head_others, seq_partner):
    s = lax.axis_index("seq")
    z = s // 2
    barrier = pltpu.get_barrier_semaphore()
    for other in head_others:
        pl.semaphore_signal(barrier, inc=1, device_id={"head": other}, device_id_type=MESH)
    pl.semaphore_signal(barrier, inc=1, device_id={"seq": seq_partner}, device_id_type=MESH)

    @pl.when(z > 0)
    def _():
        pl.semaphore_signal(barrier, inc=1, device_id={"seq": s - 2}, device_id_type=MESH)

    @pl.when(z < 3)
    def _():
        pl.semaphore_signal(barrier, inc=1, device_id={"seq": s + 2}, device_id_type=MESH)

    pl.semaphore_wait(barrier, len(head_others) + jnp.where((z > 0) & (z < 3), 3, 2))


def front_body(
    nr, heads,
    logc_ref, tok_h, cot_h, gains_ref, wq_h, wk_h, wv_h, wg_h, cos_ref, sin_ref, gg_ref,
    all_h, cot_all_h, n1_h, far_h, q_h, k_h, v_h, gate_h, ret_h, mixed_h, states_h, in_h, full_ref,
    rows_v, wq, wk, wv, wg, q_v, k_v, v_v, gate_v, ret_v, mixed_v, states, state, s_in, s_n1,
    load_sem, y_sem, c_sem, d_sem, sent_sem, cot_sem, cot_sent, gain_sem, gain_sent, share_sem, shared_sem,
    hand_sem, out_sem, mix_sem,
    *carry,
):
    h = lax.axis_index("head")
    y, c = h // 2, h % 2
    sibling, across = h + 1 - 2 * c, h + 2 - 4 * y
    s = lax.axis_index("seq")
    partner = s + 1 - 2 * (s % 2)
    T, D = rows_v.shape
    half, cols = D // 2, D // 4
    real = wv_h.shape[0] // heads
    per_block = BLK // ROWS

    def at(r):
        return pl.ds(pl.multiple_of(r * ROWS, ROWS), ROWS)

    def block(i):
        return pl.ds(pl.multiple_of(i * cols, 128), cols)

    def remote(src, dst, sent, got, **to):
        return pltpu.make_async_remote_copy(
            src_ref=src, dst_ref=dst, send_sem=sent, recv_sem=got, device_id=to, device_id_type=MESH,
        )

    def landed(ref, sem):
        pltpu.make_async_copy(ref, ref, sem).wait()

    greet((sibling, across), partner)

    def to_across(r):
        return remote(tok_h.at[at(r)], rows_v.at[at(r), block(h)], sent_sem.at[0], y_sem.at[r], head=across)

    def to_sibling(r):
        return remote(tok_h.at[at(r)], rows_v.at[at(r), block(h)], sent_sem.at[1], c_sem.at[r], head=sibling)

    gain_own = gains_ref
    gain_y = remote(gain_own, full_ref.at[:, block(h)], gain_sent.at[0], gain_sem.at[0], head=across)
    gain_c = remote(gain_own, full_ref.at[:, block(h)], gain_sent.at[1], gain_sem.at[1], head=sibling)
    gain_d = remote(
        full_ref.at[:, block(across)], full_ref.at[:, block(across)], gain_sent.at[2], gain_sem.at[2], head=sibling
    )
    gain_y.start()
    gain_c.start()
    own_tokens = pltpu.make_async_copy(tok_h, rows_v.at[:, block(h)], load_sem.at[0])
    own_tokens.start()
    for r in range(nr):
        to_across(r).start()
        to_sibling(r).start()
    loads = [
        pltpu.make_async_copy(wq_h, wq, load_sem.at[1]), pltpu.make_async_copy(wk_h, wk, load_sem.at[2])
    ]
    for k, (src, dst) in enumerate([(wv_h, wv), (wg_h, wg)]):
        for i in range(heads):
            loads.append(
                pltpu.make_async_copy(
                    src.at[pl.ds(i * real, real)], dst.at[pl.ds(i * DVP, real)], load_sem.at[3 + k * heads + i]
                )
            )
    for load in loads:
        load.start()
    own_cot = pltpu.make_async_copy(cot_h, cot_all_h.at[:, block(h)], load_sem.at[3 + 2 * heads])
    own_cot.start()
    cot_y = remote(cot_h, cot_all_h.at[:, block(h)], cot_sent.at[0], cot_sem.at[0], head=across)
    cot_c = remote(cot_h, cot_all_h.at[:, block(h)], cot_sent.at[1], cot_sem.at[1], head=sibling)
    far_block = cot_all_h.at[:, block(across)]
    cot_d = remote(far_block, far_block, cot_sent.at[2], cot_sem.at[2], head=sibling)
    for dst in (wv, wg):
        for i in range(heads):
            dst[i * DVP + real : (i + 1) * DVP, :] = jnp.zeros((DVP - real, D), BF16)
    full_ref[:, block(h)] = gains_ref[...]
    state[...] = jnp.zeros_like(state)
    gain_y.wait_recv()
    gain_d.start()
    gain_c.wait_recv()
    gain_d.wait_recv()
    own_tokens.wait()

    mine = pl.ds(pl.multiple_of(c * half, 128), half)

    def share(r):
        slot = lax.rem(r, 2)
        return remote(
            s_n1.at[slot, :, mine], far_h.at[at(r), mine], shared_sem.at[slot], share_sem.at[r], seq=partner
        )

    def hand(r):
        here = far_h.at[at(r), mine]
        return remote(here, here, hand_sem.at[0], hand_sem.at[1], head=sibling)

    def keep(r):
        slot = lax.rem(r, 2)
        return pltpu.make_async_copy(s_n1.at[slot], n1_h.at[at(r)], out_sem.at[slot])

    def step(t, carried):
        @pl.when(t < nr)
        def _():
            here = rows_v.at[at(t), block(across)]
            landed(here, y_sem.at[t])
            remote(here, here, sent_sem.at[2], d_sem.at[t], head=sibling).start()

        @pl.when(t == nr - 2)
        def _():
            cot_y.start()
            cot_c.start()

        r = t - 1

        @pl.when(r == 0)
        def _():
            for load in loads:
                load.wait()

        @pl.when((r >= 0) & (r < nr))
        def _():
            slot = lax.rem(r, 2)
            landed(rows_v.at[at(r), block(sibling)], c_sem.at[r])
            diag = lax.rem(sibling + 2, 4)
            landed(rows_v.at[at(r), block(diag)], d_sem.at[r])
            normal, _ = row_stats(rows_v[at(r), :].astype(F32), 1e-05)
            normed = (normal * full_ref[0:1, :]).astype(BF16)

            @pl.when(r >= 2)
            def _():
                keep(r).wait()
                share(r).wait_send()

            s_n1[slot] = normed
            keep(r).start()
            share(r).start()
            query = jnp.dot(normed, wq[...], preferred_element_type=F32)
            key = jnp.dot(normed, wk[...], preferred_element_type=F32)
            value = contract(normed, wv[...], 1, 1).astype(BF16)
            v_v[at(r), :] = value
            gate_v[at(r), :] = contract(normed, wg[...], 1, 1)
            cosine, sine = cos_ref[at(r), :], sin_ref[at(r), :]
            o = lax.broadcasted_iota(jnp.int32, (ROWS, 1), 0).astype(F32)
            for i in range(heads):
                logc = logc_ref[i]
                keys = slice(i * DK, (i + 1) * DK)
                q_v[at(r), keys] = turn(query[:, keys], cosine, sine).astype(BF16)
                low = (turn(key[:, keys], cosine, sine) * (1.0 / math.sqrt(DK))).astype(BF16)
                k_v[at(r), keys] = low
                scaled = (low.astype(F32) * jnp.exp((ROWS - 1.0 - o) * logc)).astype(BF16)
                new = contract(scaled, value[:, i * DVP : (i + 1) * DVP], 0, 0)
                state[i] = decay_row(logc, DVP, float(ROWS)) * state[i] + new

            @pl.when(lax.rem(r, per_block) == per_block - 1)
            def _():
                states[r // per_block] = state[...]

        g = t - 3

        @pl.when(g >= 0)
        def _():
            here = far_h.at[at(g), mine]
            landed(here, share_sem.at[g])
            hand(g).start()

        return carried

    begin, end = carry_state(False, logc_ref, T, state, s_in, carry[:4], carry[4:])
    lax.fori_loop(0, nr + 1, step, 0)
    begin()
    outs = [
        pltpu.make_async_copy(src, dst, out_sem.at[2 + i])
        for i, (src, dst) in enumerate(
            [(rows_v, all_h), (q_v, q_h), (k_v, k_h), (v_v, v_h), (gate_v, gate_h), (states, states_h)]
        )
    ]
    for copy in outs:
        copy.start()
    cot_y.wait_recv()
    cot_d.start()

    nb = T // BLK
    for i in range(heads):
        mask = decay_square(logc_ref[i])
        for b in range(nb):
            keys, vals = slice(i * DK, (i + 1) * DK), slice(i * DVP, (i + 1) * DVP)
            scores = contract(q_v[rows(b), keys], k_v[rows(b), keys], 1, 1)
            weights = (scores * mask).astype(BF16)
            ret_v[rows(b), vals] = jnp.dot(weights, v_v[rows(b), vals], preferred_element_type=F32)
    end()
    keep_in = pltpu.make_async_copy(s_in, in_h, out_sem.at[8])
    keep_in.start()
    tail = []
    for i in range(heads):
        logc = logc_ref[i]
        into = jnp.exp((offsets() + 1.0) * logc)
        for b in range(nb):
            keys, vals = slice(i * DK, (i + 1) * DK), slice(i * DVP, (i + 1) * DVP)
            total = s_in[i] if b == 0 else decay_row(logc, DVP, float(b * BLK)) * s_in[i] + states[b - 1, i]
            scaled = (q_v[rows(b), keys].astype(F32) * into).astype(BF16)
            retained = ret_v[rows(b), vals] + jnp.dot(
                scaled, total.astype(BF16), preferred_element_type=F32
            )
            ret_v[rows(b), vals] = retained
            ohat, _ = group_stats(retained)
            gate = gate_v[rows(b), vals]
            act = gate * jax.nn.sigmoid(gate)
            mixed_v[rows(b), vals] = (act * (ohat * gg_ref[:, vals])).astype(BF16)
            for k, (src, dst) in enumerate([(ret_v, ret_h), (mixed_v, mixed_h)]):
                copy = pltpu.make_async_copy(
                    src.at[rows(b), vals], dst.at[rows(b), vals], mix_sem.at[k, i * nb + b]
                )
                copy.start()
                tail.append(copy)

    for copy in outs + tail + [keep_in, own_cot]:
        copy.wait()
    lax.fori_loop(nr + 1, nr + 3, step, 0)
    for slot in range(2):
        keep(slot).wait()
        share(slot).wait_send()
    other = far_h.at[:, pl.ds(pl.multiple_of((1 - c) * half, 128), half)]
    landed(other, hand_sem.at[0])
    landed(other, hand_sem.at[1])
    own_columns = rows_v.at[:, block(h)]
    for k in range(3):
        landed(own_columns, sent_sem.at[k])
    gain_y.wait_send()
    gain_c.wait_send()
    gain_d.wait_send()
    cot_c.wait_recv()
    cot_d.wait_recv()
    cot_y.wait_send()
    cot_c.wait_send()
    cot_d.wait_send()


def front_kernel(
    logc, tokens, cotangent, gains, w_query, w_key, wv, wg, cosine, sine, group_gain, heads
):
    T, cols = tokens.shape
    D, nr, nb = 4 * cols, T // ROWS, T // BLK
    keys, vals = heads * DK, heads * DVP
    low = functools.partial(jax.ShapeDtypeStruct, dtype=BF16)
    wide = functools.partial(jax.ShapeDtypeStruct, dtype=F32)
    anywhere, vmem = pl.BlockSpec(memory_space=pl.ANY), pl.BlockSpec(memory_space=pltpu.VMEM)
    dma = pltpu.SemaphoreType.DMA
    return pl.pallas_call(
        functools.partial(front_body, nr, heads),
        out_shape=[
            low((T, D)), low((T, D)), low((T, D)), low((T, D)), low((T, keys)), low((T, keys)),
            low((T, vals)), wide((T, vals)), wide((T, vals)), low((T, vals)),
            wide((nb, heads, DK, DVP)), wide((heads, DK, DVP)), wide((8, D)),
        ],
        in_specs=[pl.BlockSpec(memory_space=pltpu.SMEM)] + [anywhere] * 2 + [vmem] + [anywhere] * 4 + [vmem] * 3,
        out_specs=[anywhere] * 12 + [vmem],
        scratch_shapes=[
            pltpu.VMEM((T, D), BF16), pltpu.VMEM((D, keys), BF16), pltpu.VMEM((D, keys), BF16),
            pltpu.VMEM((vals, D), BF16), pltpu.VMEM((vals, D), BF16),
            pltpu.VMEM((T, keys), BF16), pltpu.VMEM((T, keys), BF16), pltpu.VMEM((T, vals), BF16),
            pltpu.VMEM((T, vals), F32), pltpu.VMEM((T, vals), F32), pltpu.VMEM((T, vals), BF16),
            pltpu.VMEM((nb, heads, DK, DVP), F32), pltpu.VMEM((heads, DK, DVP), F32),
            pltpu.VMEM((heads, DK, DVP), F32), pltpu.VMEM((2, ROWS, D), BF16),
            dma((4 + 2 * heads,)), dma((nr,)), dma((nr,)), dma((nr,)), dma((3,)), dma((3,)), dma((3,)),
            dma((3,)), dma((3,)), dma((nr,)), dma((2,)), dma((2,)), dma((9,)), dma((2, heads * nb)),
        ] + carry_scratch(),
        compiler_params=pltpu.CompilerParams(
            collective_id=2, has_side_effects=True, vmem_limit_bytes=60 * 2**20
        ),
        cost_estimate=pl.CostEstimate(
            flops=2 * T * D * 2 * (keys + vals), bytes_accessed=60 * 2**20, transcendentals=T * vals
        ),
        name="tokens_to_mixed",
    )(logc, tokens, cotangent, gains, w_query, w_key, wv, wg, cosine, sine, group_gain)


def back_body(
    nr, heads,
    logc_ref, db_h, wo_h, ret_h, gate_h, gg_ref, q_h, k_h, v_h, states_h, in_h, cos_ref, sin_ref,
    wq_h, wk_h, wv_h, wg_h, tok_h, gain_ref, dr_h, chip_h,
    near_h, far_h, sums_h, gg_grad_ref, gt_h, ng_ref,
    rows_v, big, wq, wk, wg, ret, gate, q_v, k_v, v_v, states, s_in, dr_v,
    dg, dret, dq, dk, dv, ds, later, s_gt,
    side, side_give, side_far,
    load_sem, late_sem, act_sem, act_sent, sums_sem, near_sem, gt_sem, side_sem, side_sent, side_got, side_gone,
    *rest,
):
    carry, scatter = rest[:8], rest[8:]
    h = lax.axis_index("head")
    y, c = h // 2, h % 2
    sibling, across = h + 1 - 2 * c, h + 2 - 4 * y
    s = lax.axis_index("seq")
    x = s % 2
    partner = s + 1 - 2 * x
    T, D = rows_v.shape
    real = wo_h.shape[0] // heads
    nb = T // BLK

    def at(r):
        return pl.ds(pl.multiple_of(r * ROWS, ROWS), ROWS)

    def padded(src, dst, sems, k):
        return [
            pltpu.make_async_copy(src.at[pl.ds(i * real, real)], dst.at[pl.ds(i * DVP, real)], sems.at[k + i])
            for i in range(heads)
        ]

    early = [pltpu.make_async_copy(db_h, rows_v, load_sem.at[0])] + padded(wo_h, big, load_sem, 1)
    pairs = [(ret_h, ret), (gate_h, gate), (q_h, q_v), (k_h, k_v), (v_h, v_v), (states_h, states), (in_h, s_in)]
    pairs += [(wq_h, wq), (wk_h, wk), (dr_h, dr_v)]
    others = [
        pltpu.make_async_copy(src, dst, load_sem.at[1 + heads + i]) for i, (src, dst) in enumerate(pairs)
    ] + padded(wg_h, wg, load_sem, 1 + heads + len(pairs))
    for load in early + others:
        load.start()
    for dst in (big, wg):
        for i in range(heads):
            dst[i * DVP + real : (i + 1) * DVP, :] = jnp.zeros((DVP - real, D), BF16)
    greet((sibling, across), partner)
    mlp = pltpu.make_async_remote_copy(
        src_ref=chip_h.at[:, pl.ds(0, D // 4)], dst_ref=sums_h, send_sem=sums_sem.at[0], recv_sem=sums_sem.at[1],
        device_id={"head": across}, device_id_type=MESH,
    )
    mlp.start()
    for load in early + others[:3]:
        load.wait()

    def send_half(k, value, place, width):
        stay = pltpu.make_async_copy(
            value.at[:, pl.ds(pl.multiple_of(x * width, 128), width)], near_h.at[:, pl.ds(place, width)],
            near_sem.at[k],
        )
        go = pltpu.make_async_remote_copy(
            src_ref=value.at[:, pl.ds(pl.multiple_of((1 - x) * width, 128), width)],
            dst_ref=far_h.at[:, pl.ds(place, width)], send_sem=act_sent.at[k], recv_sem=act_sem.at[k],
            device_id={"seq": partner}, device_id_type=MESH,
        )
        stay.start()
        go.start()
        return stay, go

    for i in range(heads):
        logc = logc_ref[i]
        into = jnp.exp((offsets() + 1.0) * logc)
        keys, vals = slice(i * DK, (i + 1) * DK), slice(i * DVP, (i + 1) * DVP)
        gain = gg_ref[:, vals]
        for b in range(nb):
            dmixed = contract(rows_v[rows(b), :], big[vals, :], 1, 1)
            g = gate[rows(b), vals]
            ohat, inverse = group_stats(ret[rows(b), vals])
            sig = jax.nn.sigmoid(g)
            dgrouped = dmixed * (g * sig)
            dg[rows(b), vals] = (dmixed * (ohat * gain) * sig * (1.0 + g * (1.0 - sig))).astype(BF16)
            total = jnp.sum(dgrouped * ohat, axis=0, keepdims=True)
            e = dgrouped * gain
            mean = jnp.sum(e, axis=1, keepdims=True) * (1.0 / DV)
            cross = jnp.sum(e * ohat, axis=1, keepdims=True) * (1.0 / DV)
            inside = lax.broadcasted_iota(jnp.int32, e.shape, 1) < DV
            low = jnp.where(inside, inverse * (e - mean - ohat * cross), 0.0).astype(BF16)
            dret[rows(b), vals] = low
            scaled = (q_v[rows(b), keys].astype(F32) * into).astype(BF16)
            new = contract(scaled, low, 0, 0)
            if b == 0:
                gg_grad_ref[:, vals] = total
                ds[i] = new
            else:
                gg_grad_ref[:, vals] += total
                ds[i] += decay_row(logc, DVP, float(b * BLK)) * new
    begin, end = carry_state(True, logc_ref, T, ds, later, carry[:4], carry[4:])
    begin()
    halves = []
    tokens_in = pltpu.make_async_copy(tok_h, rows_v, late_sem.at[0])
    values_in = padded(wv_h, big, late_sem, 1)
    tokens_in.start()
    for load in values_in:
        load.start()
    for load in others[3:]:
        load.wait()

    for i in range(heads):
        logc = logc_ref[i]
        mask = decay_square(logc)
        into = jnp.exp((offsets() + 1.0) * logc)
        keys, vals = slice(i * DK, (i + 1) * DK), slice(i * DVP, (i + 1) * DVP)
        for b in range(nb):
            query, key = q_v[rows(b), keys], k_v[rows(b), keys]
            value, low = v_v[rows(b), vals], dret[rows(b), vals]
            weights = (contract(query, key, 1, 1) * mask).astype(BF16)
            dweights = (contract(low, value, 1, 1) * mask).astype(BF16)
            state = s_in[i] if b == 0 else decay_row(logc, DVP, float(b * BLK)) * s_in[i] + states[b - 1, i]
            dquery = jnp.dot(dweights, key, preferred_element_type=F32)
            dquery = dquery + contract(low, state.astype(BF16), 1, 1) * into
            dq[rows(b), keys] = turn(dquery, cos_ref[rows(b), :], -sin_ref[rows(b), :]).astype(BF16)
            gate[rows(b), keys] = contract(dweights, query, 0, 0)
            ret[rows(b), vals] = contract(weights, low, 0, 0)
    halves.append(send_half(0, dg, 0, DVP))
    halves.append(send_half(1, dq, 2 * DVP, DK))
    end()
    for i in range(heads):
        logc = logc_ref[i]
        o = offsets()
        into, to_end = jnp.exp((o + 1.0) * logc), jnp.exp((BLK - 1.0 - o) * logc)
        keys, vals = slice(i * DK, (i + 1) * DK), slice(i * DVP, (i + 1) * DVP)
        after = later[i]
        for b in reversed(range(nb)):
            low = after.astype(BF16)
            dkey = gate[rows(b), keys] + contract(v_v[rows(b), vals], low, 1, 1) * to_end
            scaled = (k_v[rows(b), keys].astype(F32) * to_end).astype(BF16)
            dvalue = ret[rows(b), vals] + jnp.dot(scaled, low, preferred_element_type=F32)
            turned = turn(dkey, cos_ref[rows(b), :], -sin_ref[rows(b), :])
            dk[rows(b), keys] = (turned * (1.0 / math.sqrt(DK))).astype(BF16)
            dv[rows(b), vals] = dvalue.astype(BF16)
            if b > 0:
                qs = (q_v[rows(b), keys].astype(F32) * into).astype(BF16)
                after = decay_row(logc, DVP, float(BLK)) * after + contract(qs, dret[rows(b), vals], 0, 0)
    halves.append(send_half(2, dv, DVP, DVP))
    halves.append(send_half(3, dk, 2 * DVP + DK, DK))
    tokens_in.wait()
    for load in values_in:
        load.wait()

    spread, collect, pass_on, gather, drain_near, drain = reduce_scatter(scatter)
    ng_ref[...] = jnp.zeros_like(ng_ref)

    def side_copy(src, dst, sent, got, to):
        return pltpu.make_async_remote_copy(
            src_ref=src, dst_ref=dst, send_sem=sent, recv_sem=got, device_id={"head": to}, device_id_type=MESH,
        )

    def put(r):
        slot = lax.rem(r, 2)
        return pltpu.make_async_copy(s_gt.at[slot], gt_h.at[at(r)], gt_sem.at[slot])

    def step(t, carried):
        r1 = t - 1

        @pl.when((r1 >= 0) & (r1 < nr))
        def _():
            collect(r1)
            pass_on(r1)
            here = side.at[at(r1)]
            pltpu.make_async_copy(here, here, side_sem.at[r1]).wait()
            side_give[at(r1), :] += side[at(r1), :]
            side_copy(side_give.at[at(r1)], side_far.at[at(r1)], side_gone, side_got.at[r1], across).start()

        g = t - 2

        @pl.when(g >= 0)
        def _():
            grad = gather(g)
            here = side_far.at[at(g)]
            pltpu.make_async_copy(here, here, side_got.at[g]).wait()
            sums = (side_give[at(g), :] + side_far[at(g), :]) * (1.0 / D)
            normal, inverse = row_stats(rows_v[at(g), :].astype(F32), 1e-05)
            normal = own_block(normal)
            ng_ref[...] += jnp.sum(grad * normal, axis=0, keepdims=True)
            e = grad * own_block(gain_ref[0:1, :])
            result = dr_v[at(g), :] + inverse * (e - (sums[:, 0:1] + normal * sums[:, 1:2]))

            @pl.when(g >= 2)
            def _():
                put(g).wait()

            s_gt[lax.rem(g, 2)] = result.astype(BF16)
            put(g).start()

        @pl.when(t < nr)
        def _():
            terms = contract(dq[at(t), :], wq[...], 1, 1) + contract(dk[at(t), :], wk[...], 1, 1)
            terms = terms + jnp.dot(dv[at(t), :], big[...], preferred_element_type=F32)
            terms = terms + jnp.dot(dg[at(t), :], wg[...], preferred_element_type=F32)
            spread(t, terms)
            normal, _ = row_stats(rows_v[at(t), :].astype(F32), 1e-05)
            weighted = terms * gain_ref[0:1, :]
            plain = jnp.sum(weighted, axis=1, keepdims=True)
            cross = jnp.sum(weighted * normal, axis=1, keepdims=True)
            lane = lax.broadcasted_iota(jnp.int32, (ROWS, 128), 1)
            side_give[at(t), :] = jnp.where(lane == 0, plain, jnp.where(lane == 1, cross, 0.0))
            side_send(t).start()

        return carried

    def side_send(r):
        return side_copy(side_give.at[at(r)], side.at[at(r)], side_sent.at[r], side_sem.at[r], sibling)

    def guarded(t, carried):
        r1 = t - 1

        @pl.when((r1 >= 0) & (r1 < nr))
        def _():
            side_send(r1).wait_send()

        return step(t, carried)

    lax.fori_loop(0, nr + 2, guarded, 0)

    drain()
    pltpu.make_async_copy(side_give, side_far, side_gone).wait()
    for slot in range(2):
        put(slot).wait()
    for stay, go in halves:
        stay.wait()
        go.wait_send()
        go.wait_recv()
    mlp.wait()


def back_kernel(
    logc, grad_branch, w_output, retained, gate, group_gain, query, key, value, states, incoming,
    cosine, sine, w_query, w_key, wv, wg, all_tokens, gains, own_resid_grad, chip_sums, heads,
):
    T, D = all_tokens.shape
    cols, nr, nb = D // 4, T // ROWS, T // BLK
    keys, vals = heads * DK, heads * DVP
    low = functools.partial(jax.ShapeDtypeStruct, dtype=BF16)
    wide = functools.partial(jax.ShapeDtypeStruct, dtype=F32)
    anywhere, vmem = pl.BlockSpec(memory_space=pl.ANY), pl.BlockSpec(memory_space=pltpu.VMEM)
    dma = pltpu.SemaphoreType.DMA
    return pl.pallas_call(
        functools.partial(back_body, nr, heads),
        out_shape=[
            low((T, DVP * 2 + DK * 2)), low((T, DVP * 2 + DK * 2)), low((T, cols)),
            wide((1, vals)), low((T, cols)), wide((1, cols)),
        ],
        in_specs=[pl.BlockSpec(memory_space=pltpu.SMEM)] + [anywhere] * 4 + [vmem] + [anywhere] * 5
        + [vmem] * 2 + [anywhere] * 5 + [vmem, anywhere, anywhere],
        out_specs=[anywhere, anywhere, anywhere, vmem, anywhere, vmem],
        scratch_shapes=[
            pltpu.VMEM((T, D), BF16), pltpu.VMEM((vals, D), BF16), pltpu.VMEM((D, keys), BF16),
            pltpu.VMEM((D, keys), BF16), pltpu.VMEM((vals, D), BF16),
            pltpu.VMEM((T, vals), F32), pltpu.VMEM((T, vals), F32),
            pltpu.VMEM((T, keys), BF16), pltpu.VMEM((T, keys), BF16), pltpu.VMEM((T, vals), BF16),
            pltpu.VMEM((nb, heads, DK, DVP), F32), pltpu.VMEM((heads, DK, DVP), F32),
            pltpu.VMEM((T, cols), F32),
            pltpu.VMEM((T, vals), BF16), pltpu.VMEM((T, vals), BF16), pltpu.VMEM((T, keys), BF16),
            pltpu.VMEM((T, keys), BF16), pltpu.VMEM((T, vals), BF16),
            pltpu.VMEM((heads, DK, DVP), F32), pltpu.VMEM((heads, DK, DVP), F32),
            pltpu.VMEM((2, ROWS, cols), BF16),
            pltpu.VMEM((T, 128), F32), pltpu.VMEM((T, 128), F32), pltpu.VMEM((T, 128), F32),
            dma((11 + 2 * heads,)), dma((1 + heads,)), dma((4,)), dma((4,)), dma((2,)), dma((4,)), dma((2,)),
            dma((nr,)), dma((nr,)), dma((nr,)), dma,
        ] + carry_scratch() + scatter_scratch(T, D),
        compiler_params=pltpu.CompilerParams(
            collective_id=3, has_side_effects=True, vmem_limit_bytes=63 * 2**20
        ),
        cost_estimate=pl.CostEstimate(
            flops=2 * T * D * (2 * keys + 3 * vals), bytes_accessed=50 * 2**20, transcendentals=T * vals
        ),
        name="dbranch_to_grad_tokens",
    )(
        logc, grad_branch, w_output, retained, gate, group_gain, query, key, value, states, incoming,
        cosine, sine, w_query, w_key, wv, wg, all_tokens, gains, own_resid_grad, chip_sums,
    )


def pad_cols(w, parts):
    w = w.reshape(w.shape[0], parts, w.shape[1] // parts)
    fill = -w.shape[2] % 128
    return jnp.pad(w, ((0, 0), (0, 0), (0, fill))).reshape(w.shape[0], -1)


def pad_rows(w, parts):
    w = w.reshape(parts, w.shape[0] // parts, w.shape[1])
    fill = -w.shape[1] % 128
    return jnp.pad(w, ((0, 0), (0, fill), (0, 0))).reshape(-1, w.shape[2])


def unpad_rows(w, parts, real):
    return w.reshape(parts, -1, w.shape[1])[:, : real // parts].reshape(real, w.shape[1])


def seq_sum(grads):
    return [g.astype(F32) for g in lax.psum([g.astype(BF16) for g in grads], "seq")]


def unpad_cols(w, heads):
    return w.reshape(w.shape[0], heads, DVP)[:, :, :DV].reshape(w.shape[0], heads * DV)


def per_device(
    tokens,
    norm_gain,
    w_query,
    w_key,
    w_value,
    w_gate,
    group_gain,
    w_output,
    mlp_gain,
    w_first,
    w_second,
    w_third,
    cotangent,
):
    T, cols = tokens.shape
    heads = w_query.shape[1] // DK
    fast = lax.axis_size("seq") == 8 and lax.axis_size("head") == 4
    head_rank = lax.axis_index("head")
    seq_rank = lax.axis_index("seq")
    features = cols * lax.axis_size("head")

    units, values = w_first.shape[1], w_value.shape[1]
    if not fast:
        wv, wg, wo = pad_rows(w_value.T, heads), pad_rows(w_gate.T, heads), pad_rows(w_output, heads)
    gain = pad_cols(group_gain.astype(F32)[None], heads)

    positions = (seq_rank * T + jnp.arange(T)).astype(F32)
    frequency = 10000.0 ** (-jnp.arange(DK // 2, dtype=F32) / (DK // 2 - 1))
    angles = positions[:, None] * frequency[None, :]
    cosine, sine = jnp.cos(angles), jnp.sin(angles)
    head_ids = (head_rank * heads + jnp.arange(heads)).astype(F32)
    logc = jnp.log(1.0 - jnp.exp2(-5.0 - head_ids))
    factor = jnp.exp(T * logc)

    if fast:
        gains = jnp.concatenate([norm_gain[None], mlp_gain[None], jnp.zeros((6, cols), BF16)]).astype(F32)
        (
            all_tokens, all_cot, normed, far_normed, query, key, value, gate, retained, mixed, states,
            incoming, gains,
        ) = front_kernel(
            logc, tokens, cotangent, gains, w_query, w_key, w_value.T, w_gate.T, cosine, sine, gain, heads
        )
        full_mlp_gain = gains[1]
    else:
        gains = lax.all_gather(jnp.stack([norm_gain, mlp_gain]), "head", axis=1, tiled=True).astype(F32)
        full_gain, full_mlp_gain = gains[0], gains[1]
        all_tokens = lax.all_gather(tokens, "head", axis=1, tiled=True)
        all_cot = lax.all_gather(cotangent, "head", axis=1, tiled=True)
        normal_in, inverse_in = row_stats(all_tokens.astype(F32), 1e-05)
        normed = (normal_in * full_gain).astype(BF16)
        query_raw = jnp.dot(normed, w_query, preferred_element_type=F32)
        key_raw = jnp.dot(normed, w_key, preferred_element_type=F32)
        value = contract(normed, wv, 1, 1).astype(BF16)
        gate = contract(normed, wg, 1, 1)
        query, key, states = per_head(
            fwd_state_kernel, heads, T,
            ["smem", "key", "key", "val", "rot", "rot"],
            [("key", BF16), ("key", BF16), ("states", F32)],
            "retention_state",
        )(logc, query_raw, key_raw, value, cosine, sine)
        incoming = seq_carry(states[-1], factor, False)
        mixed, retained = per_head(
            fwd_out_kernel, heads, T,
            ["smem", "key", "key", "val", "states", "state", "val", "gain"],
            [("val", BF16), ("val", F32)],
            "retention_out",
        )(logc, query, key, value, states, incoming, gate, gain)

    middle = middle_kernel if fast else middle_general
    (
        normed_two, hidden, grad_up_one, grad_up_two, output, chip_sums, grad_branch, own_resid_grad, far_two,
        far_up_one, far_up_two, mlp_gain_grad,
    ) = middle(
        mixed, all_tokens, all_cot, w_output, w_first.T, w_second.T, w_third, full_mlp_gain[None], heads,
    )
    grad_mlp_gain = lax.dynamic_slice_in_dim(mlp_gain_grad[0], head_rank * cols, cols)

    if fast:
        near, far, far_sums, group_gain_grad, grad_tokens, grad_norm_gain = back_kernel(
            logc, grad_branch, w_output, retained, gate, gain, query, key, value, states, incoming,
            cosine, sine, w_query, w_key, w_value.T, w_gate.T, all_tokens, gains, own_resid_grad, chip_sums, heads,
        )
        output = output + (chip_sums[:, cols:].astype(F32) + far_sums.astype(F32))
        small = jnp.concatenate([grad_norm_gain[0], group_gain_grad[0], grad_mlp_gain])[None].astype(BF16)
        full = chain_sum(
            jnp.pad(small, ((0, 15), (0, 0))), hidden, all_cot, mixed, grad_branch, grad_up_one, grad_up_two,
            far_up_one, far_up_two, normed_two, far_two, near, far, normed, far_normed,
        )
        (
            small, grad_third, grad_first, grad_second, grad_output, grad_gate, grad_value, grad_query, grad_key,
        ) = finish(full, [(i * DV, DV, False) for i in range(2, 7)] + [(7 * DV, DK, True), (7 * DV + DK, DK, True)])
        small = small[0]
    else:
        grad_mixed = contract(grad_branch, wo, 1, 1)
        grad_gate_rows, grad_ret, group_gain_grad, state_grad = per_head(
            bwd_mix_kernel, heads, T,
            ["smem", "val", "val", "val", "gain", "key"],
            [("val", BF16), ("val", BF16), ("gain", F32), ("state", F32)],
            "mix_backward",
        )(logc, grad_mixed, retained, gate, gain, query)
        outgoing = seq_carry(state_grad, factor, True)
        grad_query_raw, grad_key_raw, grad_value_rows = per_head(
            bwd_ret_kernel, heads, T,
            ["smem", "key", "key", "val", "val", "states", "state", "state", "rot", "rot"],
            [("key", BF16), ("key", BF16), ("val", BF16)],
            "retention_backward",
        )(logc, query, key, value, grad_ret, states, incoming, outgoing, cosine, sine)
        input_terms = (
            contract(grad_query_raw, w_query, 1, 1)
            + contract(grad_key_raw, w_key, 1, 1)
            + jnp.dot(grad_value_rows, wv, preferred_element_type=F32)
            + jnp.dot(grad_gate_rows, wg, preferred_element_type=F32)
        )
        grad_normed = head_reduce_scatter(input_terms)
        weighted = input_terms * full_gain
        sums = lax.psum(
            jnp.stack([jnp.sum(weighted, axis=1), jnp.sum(weighted * normal_in, axis=1)]), "head"
        )
        own_normal = lax.dynamic_slice_in_dim(normal_in, head_rank * cols, cols, axis=1)
        scaled_grad = grad_normed * norm_gain.astype(F32)
        grad_tokens = (
            own_resid_grad
            + inverse_in
            * (scaled_grad - (sums[0][:, None] + own_normal * sums[1][:, None]) / features)
        ).astype(BF16)
        grad_norm_gain = jnp.sum(grad_normed * own_normal, axis=0)
        grads = [contract(act, normed, 0, 0) for act in (grad_query_raw, grad_key_raw)]
        grads += [
            unpad_rows(contract(grad_value_rows, normed, 0, 0), heads, values),
            unpad_rows(contract(grad_gate_rows, normed, 0, 0), heads, values),
            unpad_rows(contract(mixed, grad_branch, 0, 0), heads, values),
            unpad_rows(contract(hidden, all_cot, 0, 0), heads, units),
            unpad_rows(contract(grad_up_one, normed_two, 0, 0), heads, units),
            unpad_rows(contract(grad_up_two, normed_two, 0, 0), heads, units),
        ]
        (
            grad_query, grad_key, grad_value, grad_gate, grad_output, grad_third, grad_first, grad_second,
        ) = seq_sum(grads)
        grad_query, grad_key = grad_query.T, grad_key.T
        small = lax.psum(jnp.concatenate([grad_norm_gain, group_gain_grad[0], grad_mlp_gain]), "seq")

    grad_norm_gain = small[:cols]
    grad_group_gain = unpad_cols(small[None, cols : cols + heads * DVP], heads)[0]
    grad_mlp_gain = small[cols + heads * DVP :]
    return (
        output.astype(BF16),
        grad_tokens,
        grad_norm_gain,
        grad_query,
        grad_key,
        grad_value.T,
        grad_gate.T,
        grad_group_gain,
        grad_output,
        grad_mlp_gain,
        grad_first.T,
        grad_second.T,
        grad_third,
    )


def solution(mesh):
    rows_cols, cut, columns, depth = P("seq", "head"), P("head"), P(None, "head"), P("head", None)
    return jax.shard_map(
        per_device,
        mesh=mesh,
        in_specs=(
            rows_cols, cut, columns, columns, columns, columns, cut, depth, cut,
            columns, columns, depth, rows_cols,
        ),
        out_specs=(
            rows_cols, rows_cols, cut, columns, columns, columns, columns, cut, depth, cut,
            columns, columns, depth,
        ),
        check_vma=False,
    )
```
